512 devices in a mesh: loop: 32 (over x_hi, y, core), orb: 16 (over z, x_lo).
Axes of the slice: x: 4 (x_hi: 2, x_lo: 2; x = x_hi * 2 + x_lo), y: 8, z: 8, core: 2. Of those that a mesh axis runs over, the one named last changes fastest.
Arguments:
- cholesky: bfloat16 [4096, 65536], P('loop', 'orb'), may hold values from -0.0234375 to 0.0234375
- green_half: bfloat16 [1536, 65536], P('loop', 'orb'), may hold values from -6 to 6
- partners: int32 [256, 2], replicated, may hold values from 0 to 1535, as said below
Outputs:
- green_copied: bfloat16 [1536, 65536], P('loop', 'orb')
- force_bias: float32 [1536, 4096], P('orb', 'loop')
The draws below stay inside these ranges and needn't reach their ends.
Inputs may be any that keep to these rules, and one draw needn't show every extreme that they name: `partners`: column 0 is a source walker, column 1 a destination walker. Destinations are distinct, sources are distinct, and no source is a destination. Each block of 48 consecutive walkers holds exactly 8 destinations and exactly 8 sources.
All inputs are finite; a program needn't handle non-finite values.
Results may differ from the reference program's by a relative error of at most 0.001.
Values may be sent and summed in bfloat16 or wider, within the bound.
A program may use at most 64 MiB of HBM per device.

```python
import jax
import jax.numpy as jnp
from jax import lax

NCHOL = 4096
WALK_DEV = 48
EV_DEV = 8
PAIRS = 65536
WALKERS = 1536


def draw_partners(key, part):
    blocks = WALKERS // WALK_DEV
    block_keys = jax.random.split(jax.random.fold_in(key, 11), blocks)
    orders = jax.vmap(lambda block_key: jax.random.permutation(block_key, WALK_DEV))(block_keys).astype(jnp.int32)
    base = (jnp.arange(blocks, dtype=jnp.int32) * WALK_DEV)[:, None]
    targets = (orders[:, :EV_DEV] + base).reshape(-1)
    sources = (orders[:, EV_DEV:2 * EV_DEV] + base).reshape(-1)
    pairing = jax.random.permutation(jax.random.fold_in(key, 12), blocks * EV_DEV)
    listed = jnp.stack([sources[pairing], targets], axis=1)
    shuffle = jax.random.permutation(jax.random.fold_in(key, 13), blocks * EV_DEV)
    return listed[shuffle].astype(jnp.int32)


def with_spikes(drawn, own_key, source, target, shards_of, factor):
    def block_of(position):
        return (jnp.arange(drawn.shape[position]) // (drawn.shape[position] // shards_of)).reshape((-1,) + (1,) * (drawn.ndim - 1 - position))

    one_side = jax.random.permutation(own_key, shards_of)[block_of(target)]
    second = (block_of(target) + shards_of // 2) % shards_of
    return jnp.where((block_of(source) == one_side) | (block_of(source) == second), factor * drawn, drawn)


def steps_of(rng, extent, shards, least, top_value):
    factor_of = 1.0
    for position, shards_of in shards:
        steps = jax.random.uniform(jax.random.fold_in(jax.random.fold_in(rng, 6), position), (shards_of,), jnp.float32, least / len(shards), top_value / len(shards))
        factor_of = factor_of * jnp.repeat(jnp.exp(steps), extent[position] // shards_of).reshape((-1,) + (1,) * (len(extent) - 1 - position))
    return factor_of


def noise(own_key, extent, width, reach, cuts=(), kind=jnp.bfloat16):
    entries = jax.random.normal(own_key, extent, jnp.float32) * width
    if len(cuts) > 0:
        entries = steps_of(own_key, extent, cuts, -0.22, 0.18) * entries
    return jnp.clip(entries, min=-reach, max=reach).astype(kind)


def bell_draw_with(rng, extent, scale, most, shards, heavy, kind=jnp.bfloat16):
    result = scale * jax.random.normal(rng, extent, jnp.float32)
    if shards:
        result = result * steps_of(rng, extent, shards, -0.22, 0.18)
    return jnp.clip(with_spikes(result, jax.random.fold_in(rng, 3), *heavy), -most, most).astype(kind)


def setup_inputs(seed: int = 0) -> dict:
    streams_of = jax.random.split(jax.random.key(seed), 4)
    cholesky = noise(streams_of[0], (NCHOL, PAIRS), PAIRS ** -0.5, 0.0234375, ((0, 32), (1, 16)))
    green_half = bell_draw_with(streams_of[1], (WALKERS, PAIRS), 1.0, 6.0, ((0, 32), (1, 16)), (1, 0, 32, 2.75))
    partners = draw_partners(jax.random.fold_in(streams_of[3], 71), 0)
    return dict(cholesky=cholesky, green_half=green_half, partners=partners)


def reference(cholesky, green_half, partners):
    green_copied = green_half.at[partners[:, 1]].set(green_half[partners[:, 0]])

    def block_bias(walker_rows):
        return lax.dot_general(walker_rows, cholesky, (((1,), (1,)), ((), ())), preferred_element_type=jnp.float32)

    stacked = lax.map(block_bias, green_copied.reshape(WALKERS // WALK_DEV, WALK_DEV, PAIRS))
    return green_copied, stacked.reshape(WALKERS, NCHOL)
```

```python
import jax
import jax.numpy as jnp
from jax import lax
from jax.experimental import pallas as pl
from jax.experimental.pallas import tpu as pltpu
from jax.sharding import PartitionSpec as P

MESH = pl.DeviceIdType.MESH
NY, NZ, NX = 8, 8, 4
F32, BF16 = jnp.float32, jnp.bfloat16


def dot_t(a, b):
    return lax.dot_general(a, b, (((1,), (1,)), ((), ())), preferred_element_type=F32)


def split3(v):
    hi = v.astype(BF16)
    rest = v - hi.astype(F32)
    mid = rest.astype(BF16)
    lo = (rest - mid.astype(F32)).astype(BF16)
    return hi, mid, lo


def pick_rows(onehot, v):
    hi, mid, lo = split3(v)
    return (
        jnp.dot(onehot, hi, preferred_element_type=F32)
        + jnp.dot(onehot, mid, preferred_element_type=F32)
    ) + jnp.dot(onehot, lo, preferred_element_type=F32)


def iota(shape, dim):
    return lax.broadcasted_iota(jnp.int32, shape, dim).astype(F32)


def kernel(
    chol, green, prow, new_green, bias,
    gb, w, cs, rx, zs, rz, fix, fx, rfx, fzs, rfz, s_acc, s_out, s_in, csrc, ch_out,
    y_ss, y_rs, b_ss, b_rs, p_ss, p_rs, x_ss, x_rs, z_ss, z_rs, fx_ss, fx_rs, fz_ss, fz_rs,
):
    rows = green.shape[0]
    half = green.shape[1] // 2
    vec = chol.shape[0]
    two = 2 * rows
    loop, orb = lax.axis_index("loop"), lax.axis_index("orb")
    h, y, c = lax.div(loop, 16), lax.rem(lax.div(loop, 2), NY), lax.rem(loop, 2)
    z, xl = lax.div(orb, 2), lax.rem(orb, 2)
    x = 2 * h + xl
    other = 1 - h

    def dev(dx=0, dy=0, dz=0, dc=0):
        xx = lax.rem(x + dx, NX)
        yy = lax.rem(y + dy + NY, NY)
        zz = lax.rem(z + dz, NZ)
        cc = lax.rem(c + dc, 2)
        return (lax.div(xx, 2) * 16 + yy * 2 + cc, zz * 2 + lax.rem(xx, 2))

    def remote(src, dst, ss, rs, to):
        return pltpu.make_async_remote_copy(
            src_ref=src, dst_ref=dst, send_sem=ss, recv_sem=rs, device_id=to, device_id_type=MESH
        )

    barrier = pltpu.get_barrier_semaphore()
    peers = [dev(dy=1), dev(dy=-1), dev(dc=1)]
    peers += [dev(dx=k) for k in range(1, NX)] + [dev(dz=k) for k in range(1, NZ)]
    for peer in peers:
        pl.semaphore_signal(barrier, inc=1, device_id=peer, device_id_type=MESH)

    own_cols = pl.ds(pl.multiple_of(h * half, half), half)
    far_cols = pl.ds(pl.multiple_of(other * half, half), half)
    gb[0, 0, c] = green[:, own_cols]
    s_out[0:rows] = green[:, far_cols]
    ch_out[...] = chol[:, far_cols]
    w[pl.ds(pl.multiple_of(h * vec, vec), vec)] = chol[:, own_cols]
    pl.semaphore_wait(barrier, len(peers))

    def y_copy(pq, d, step):
        return remote(
            gb.at[pq, d % NY, c], gb.at[pq, (d - step) % NY, c],
            y_ss.at[pq, 0 if step > 0 else 1, abs(d)], y_rs.at[pq, (d - step) % NY], dev(dy=step),
        )

    def b_copy(pq, d):
        return remote(
            gb.at[pq, d % NY, c], gb.at[pq, d % NY, c], b_ss.at[pq, d % NY], b_rs.at[pq, d % NY], dev(dc=1)
        )

    def b_wait(pq, d):
        remote(
            gb.at[pq, d % NY, 1 - c], gb.at[pq, d % NY, 1 - c], b_ss.at[pq, d % NY], b_rs.at[pq, d % NY], dev(dc=1)
        ).wait_recv()

    q_copy = remote(s_out.at[pl.ds(0, rows)], gb.at[1, 0, c], p_ss.at[0], p_rs.at[0], dev(dx=2))
    h_copy = remote(
        ch_out, w.at[pl.ds(pl.multiple_of(h * vec, vec), vec)], p_ss.at[1], p_rs.at[1], dev(dx=2)
    )
    h_in = remote(
        ch_out, w.at[pl.ds(pl.multiple_of(other * vec, vec), vec)], p_ss.at[1], p_rs.at[1], dev(dx=2)
    )
    started = []

    def go(copy):
        copy.start()
        started.append(copy)

    go(y_copy(0, 0, 1))
    go(y_copy(0, 0, -1))
    q_copy.start()
    go(b_copy(0, 0))

    events = prow.shape[1]
    src_row, tgt_row = prow[0:1, :].astype(F32), prow[1:2, :].astype(F32)
    diag = iota((events, events), 0) == iota((events, events), 1)
    tgt_col = jnp.sum(jnp.where(diag, tgt_row, 0.0), axis=1, keepdims=True)
    pos_row = jnp.sum(jnp.where(tgt_col < tgt_row, 1.0, 0.0), axis=0, keepdims=True)
    placed = iota((events, events), 0) == pos_row
    src_col = jnp.sum(jnp.where(placed, src_row, 0.0), axis=1, keepdims=True)
    csrc[...] = jnp.broadcast_to(src_col, csrc.shape)
    per = 8
    fix[...] = jnp.zeros_like(fix)
    s_acc[...] = jnp.zeros_like(s_acc)
    own_block = loop
    far_block = other * 16 + lax.rem(loop, 16)
    s_src = jnp.concatenate(
        [
            csrc[pl.ds(pl.multiple_of(own_block * per, per), per), :],
            csrc[pl.ds(pl.multiple_of(far_block * per, per), per), :],
        ],
        axis=0,
    )

    q_copy.wait_recv()
    go(y_copy(1, 0, 1))
    go(y_copy(1, 0, -1))
    go(b_copy(1, 0))
    q_copy.wait_send()
    go(h_copy)

    parity_here = lax.rem(y + xl, 2)

    def place(pq, d):
        hb = h if pq == 0 else other
        yb = lax.rem(y + (d % NY), NY)
        return hb, yb, 4 * hb + lax.div(yb, 2)

    def x_copy(pq, d, dx, slot):
        to = lax.div(lax.rem(x + dx, NX), 2)
        return remote(
            cs.at[pq, d % NY, to], rx.at[dx - 1, slot], x_ss.at[dx - 1, slot], x_rs.at[dx - 1, slot], dev(dx=dx)
        )

    def compute(pq, d):
        b_wait(pq, d)
        hb, yb, slot = place(pq, d)
        a = gb[pq, d % NY].reshape(two, half)
        part = dot_t(a, w[...])
        cs[pq, d % NY, 0] = part[:, :vec]
        cs[pq, d % NY, 1] = part[:, vec:]

        @pl.when(parity_here == d % 2)
        def _():
            x_copy(pq, d, 2, slot).start()

        @pl.when(parity_here != d % 2)
        def _():
            x_copy(pq, d, 1, slot).start()
            x_copy(pq, d, 3, slot).start()

        base = ((8 * hb + yb) * two).astype(F32)
        lane = iota((events, two), 1)
        oh = jnp.where(csrc[:, :two] - base == lane, 1.0, 0.0).astype(BF16)
        fix[...] += pick_rows(oh, part)
        oh_s = jnp.where(s_src[:, :two] - base == lane[:16], 1.0, 0.0).astype(BF16)
        s_acc[...] += jnp.dot(oh_s, a, preferred_element_type=F32)

    def z_stage(pq, d):
        _, _, slot = place(pq, d)

        @pl.when(parity_here == d % 2)
        def _():
            for dx in range(1, NX):
                x_copy(pq, d, dx, slot).wait_recv()
            zs[slot] = (cs[pq, d % NY, h] + rx[0, slot]) + (rx[1, slot] + rx[2, slot])
            k = lax.rem(slot - z + NZ, NZ)

            @pl.when(k != 0)
            def _():
                remote(zs.at[slot], rz.at[k], z_ss.at[k], z_rs.at[k], dev(dz=k)).start()

    def arrive(pq, d):
        remote(gb.at[pq, d % NY, c], gb.at[pq, d % NY, c], y_ss.at[pq, 0, 0], y_rs.at[pq, d % NY], dev(dy=1)).wait_recv()

    def take(pq, d):
        arrive(pq, d)
        up_end, down_end = (4, 3) if pq == 0 else (3, 4)
        if d < 0 and -d < up_end:
            go(y_copy(pq, d, 1))
        if 0 < d < down_end:
            go(y_copy(pq, d, -1))
        go(b_copy(pq, d))

    take(0, -1)
    take(0, 1)
    take(1, -1)
    take(1, 1)
    take(0, -2)
    take(0, 2)
    h_in.wait_recv()
    compute(0, 0)
    compute(1, 0)
    take(1, -2)
    take(1, 2)
    for d in (-1, 1):
        compute(0, d)
        compute(1, d)
    take(0, -3)
    take(0, 3)
    z_stage(0, 0)
    z_stage(1, 0)
    compute(0, -2)
    compute(0, 2)
    take(1, -3)
    take(1, 3)
    compute(1, -2)
    compute(1, 2)
    for d in (-1, 1):
        z_stage(0, d)
        z_stage(1, d)
    compute(0, -3)
    compute(0, 3)
    take(0, -4)
    take(1, 4)
    for d in (-2, 2):
        z_stage(0, d)
        z_stage(1, d)
    compute(1, -3)
    compute(1, 3)
    compute(0, 4)
    compute(1, 4)

    full = fix[...]
    for zz in range(NZ):
        for par in range(2):
            r0 = (2 * zz + par) * 16
            fx[par, 0, zz] = full[r0 : r0 + 16, :vec]
            fx[par, 1, zz] = full[r0 : r0 + 16, vec:]

    def fx_copy(dx):
        xx = lax.rem(x + dx, NX)
        return remote(fx.at[lax.rem(xx, 2), lax.div(xx, 2)], rfx.at[dx - 1], fx_ss.at[dx - 1], fx_rs.at[dx - 1], dev(dx=dx))

    for dx in range(1, NX):
        go(fx_copy(dx))
    s_out[0:16] = s_acc[...].astype(BF16)
    s_copy = remote(s_out.at[pl.ds(0, 16)], s_in, p_ss.at[2], p_rs.at[2], dev(dx=2))
    go(s_copy)
    for d in (-3, 3):
        z_stage(0, d)
        z_stage(1, d)
    z_stage(0, 4)
    z_stage(1, 4)
    for dx in range(1, NX):
        fx_copy(dx).wait_recv()
    fzs[...] = (fx[xl, h] + rfx[0]) + (rfx[1] + rfx[2])

    def fz_copy(k):
        return remote(fzs.at[lax.rem(z + k, NZ)], rfz.at[k], fz_ss.at[k], fz_rs.at[k], dev(dz=k))

    for k in range(1, NZ):
        go(fz_copy(k))

    s_copy.wait_recv()
    wide = (rows, events)
    first = (loop * rows).astype(F32)
    w_col = iota((rows, 1), 0) + first
    hit = jnp.sum(jnp.where(tgt_row == w_col, 1.0, 0.0), axis=1, keepdims=True)
    less = jnp.sum(jnp.where((tgt_row < w_col) & (tgt_row >= first), 1.0, 0.0), axis=1, keepdims=True)
    lane16 = iota((rows, 16), 1)
    put_own = jnp.where((hit > 0.5) & (less == lane16), 1.0, 0.0).astype(BF16)
    put_far = jnp.where((hit > 0.5) & (less + 8.0 == lane16), 1.0, 0.0).astype(BF16)
    keep = jnp.where((hit < 0.5) & (iota((rows, rows), 0) == iota((rows, rows), 1)), 1.0, 0.0).astype(BF16)
    new_green[:, own_cols] = (
        jnp.dot(keep, green[:, own_cols], preferred_element_type=F32)
        + jnp.dot(put_own, s_acc[...].astype(BF16), preferred_element_type=F32)
    ).astype(BF16)
    new_green[:, far_cols] = (
        jnp.dot(keep, green[:, far_cols], preferred_element_type=F32)
        + jnp.dot(put_far, s_in[...], preferred_element_type=F32)
    ).astype(BF16)

    o_first = (orb * two).astype(F32)
    o_col = iota((two, 1), 0)
    in_core = jnp.where(o_col >= rows, 1.0, 0.0)
    blk_first = o_first + in_core * rows
    o_abs = o_col + o_first
    o_hit = jnp.sum(jnp.where(tgt_row == o_abs, 1.0, 0.0), axis=1, keepdims=True)
    o_less = jnp.sum(jnp.where((tgt_row < o_abs) & (tgt_row >= blk_first), 1.0, 0.0), axis=1, keepdims=True)
    pick = jnp.where((o_hit > 0.5) & (o_less + in_core * 8.0 == iota((two, 16), 1)), 1.0, 0.0).astype(BF16)
    main = zs[z]
    tail = fzs[z]
    for k in range(1, NZ):
        remote(zs.at[0], rz.at[k], z_ss.at[k], z_rs.at[k], dev(dz=k)).wait_recv()
        main = main + rz[k]
    for k in range(1, NZ):
        fz_copy(k).wait_recv()
        tail = tail + rfz[k]
    bias[...] = jnp.where(o_hit > 0.5, pick_rows(pick, tail), main)

    for copy in started:
        copy.wait_send()
    for dx in range(1, NX):
        for slot in range(NZ):
            remote(cs.at[0, 0, 0], rx.at[dx - 1, slot], x_ss.at[dx - 1, slot], x_rs.at[dx - 1, slot], dev(dx=dx)).wait_send()
    for k in range(1, NZ):
        remote(zs.at[0], rz.at[k], z_ss.at[k], z_rs.at[k], dev(dz=k)).wait_send()


def local(cholesky, green_half, partners):
    rows, depth = green_half.shape
    vec = cholesky.shape[0]
    half, two = depth // 2, 2 * rows
    dma = pltpu.SemaphoreType.DMA
    vmem = pl.BlockSpec(memory_space=pltpu.VMEM)
    return pl.pallas_call(
        kernel,
        out_shape=(
            jax.ShapeDtypeStruct((rows, depth), BF16),
            jax.ShapeDtypeStruct((two, vec), F32),
        ),
        in_specs=[vmem] * 3,
        out_specs=(vmem, vmem),
        scratch_shapes=[
            pltpu.VMEM((2, NY, 2, rows, half), BF16),
            pltpu.VMEM((2 * vec, half), BF16),
            pltpu.VMEM((2, NY, 2, two, vec), F32),
            pltpu.VMEM((3, NZ, two, vec), F32),
            pltpu.VMEM((NZ, two, vec), F32),
            pltpu.VMEM((NZ, two, vec), F32),
            pltpu.VMEM((256, 2 * vec), F32),
            pltpu.VMEM((2, 2, NZ, 16, vec), F32),
            pltpu.VMEM((3, NZ, 16, vec), F32),
            pltpu.VMEM((NZ, 16, vec), F32),
            pltpu.VMEM((NZ, 16, vec), F32),
            pltpu.VMEM((16, half), F32),
            pltpu.VMEM((rows, half), BF16),
            pltpu.VMEM((16, half), BF16),
            pltpu.VMEM((256, 128), F32),
            pltpu.VMEM((vec, half), BF16),
            dma((2, 2, 4)), dma((2, NY)), dma((2, NY)), dma((2, NY)), dma((3,)), dma((3,)),
            dma((3, NZ)), dma((3, NZ)), dma((NZ,)), dma((NZ,)), dma((3,)), dma((3,)), dma((NZ,)), dma((NZ,)),
        ],
        compiler_params=pltpu.CompilerParams(
            collective_id=0, has_side_effects=True, vmem_limit_bytes=40 * 1024 * 1024
        ),
    )(cholesky, green_half, partners.T)


def solution(mesh):
    return jax.shard_map(
        local,
        mesh=mesh,
        in_specs=(P("loop", "orb"), P("loop", "orb"), P()),
        out_specs=(P("loop", "orb"), P("orb", "loop")),
        check_vma=False,
    )
```

```python
import jax
import jax.numpy as jnp
from jax import lax
from jax.experimental import pallas as pl
from jax.experimental.pallas import tpu as pltpu
from jax.sharding import PartitionSpec as P

MESH = pl.DeviceIdType.MESH
NY, NZ, NX = 8, 8, 4
PER = 8
F32, BF16 = jnp.float32, jnp.bfloat16


def dot_t(a, b):
    return lax.dot_general(a, b, (((1,), (1,)), ((), ())), preferred_element_type=F32)


def split3(v):
    hi = v.astype(BF16)
    rest = v - hi.astype(F32)
    mid = rest.astype(BF16)
    lo = (rest - mid.astype(F32)).astype(BF16)
    return hi, mid, lo


def pick_rows(onehot, v):
    hi, mid, lo = split3(v)
    return (
        jnp.dot(onehot, hi, preferred_element_type=F32)
        + jnp.dot(onehot, mid, preferred_element_type=F32)
    ) + jnp.dot(onehot, lo, preferred_element_type=F32)


def iota(shape, dim):
    return lax.broadcasted_iota(jnp.int32, shape, dim).astype(F32)


def kernel(
    chol, green, prow, new_green, bias,
    gv, pv, gb, w, cs, rx, zs, rz, fix, fx, rfx, fzs, rfz, s_acc, s_out, s_in, q_out, dist, in_s,
    y_ss, y_rs, b_ss, b_rs, p_ss, p_rs, x_ss, x_rs, z_ss, z_rs, fx_ss, fx_rs, fz_ss, fz_rs, near,
):
    rows = green.shape[0]
    vec = chol.shape[0]
    half = green.shape[1] // 2
    part_k = half // 2
    kept = rows - PER
    two = 2 * kept
    events = prow.shape[1]
    loop, orb = lax.axis_index("loop"), lax.axis_index("orb")
    h, y, c = lax.div(loop, 16), lax.rem(lax.div(loop, 2), NY), lax.rem(loop, 2)
    z, xl = lax.div(orb, 2), lax.rem(orb, 2)
    x = 2 * h + xl
    other = 1 - h

    def dev(dx=0, dy=0, dz=0, dc=0):
        xx = lax.rem(x + dx, NX)
        yy = lax.rem(y + dy + NY, NY)
        zz = lax.rem(z + dz + NZ, NZ)
        cc = lax.rem(c + dc, 2)
        return (lax.div(xx, 2) * 16 + yy * 2 + cc, zz * 2 + lax.rem(xx, 2))

    def remote(src, dst, ss, rs, to):
        return pltpu.make_async_remote_copy(
            src_ref=src, dst_ref=dst, send_sem=ss, recv_sem=rs, device_id=to, device_id_type=MESH
        )

    def signal(sem, to):
        pl.semaphore_signal(sem, inc=1, device_id=to, device_id_type=MESH)

    own_cols = pl.ds(pl.multiple_of(h * half, half), half)
    far_cols = pl.ds(pl.multiple_of(other * half, half), half)
    w_own = w.at[pl.ds(pl.multiple_of(h * vec, vec), vec)]
    w_far = w.at[pl.ds(pl.multiple_of(other * vec, vec), vec)]
    p_in = pltpu.make_async_copy(prow, pv, in_s.at[0])
    g_in = pltpu.make_async_copy(green, gv, in_s.at[1])
    c_in = pltpu.make_async_copy(chol.at[:, own_cols], w_own, in_s.at[2])
    p_in.start()
    g_in.start()
    c_in.start()

    barrier = pltpu.get_barrier_semaphore()
    peers = [dev(dy=1), dev(dy=-1), dev(dc=1), dev(dz=1), dev(dz=-1)] + [dev(dx=k) for k in range(1, NX)]
    for peer in peers:
        signal(barrier, peer)

    def step_near(r):
        if r > 0:
            pl.semaphore_wait(near.at[r - 1], 2)
        if r < 3:
            signal(near.at[r], dev(dz=1))
            signal(near.at[r], dev(dz=-1))

    p_in.wait()
    src_row, tgt_row = pv[0:1, :].astype(F32), pv[1:2, :].astype(F32)

    def count(first, col):
        hit = jnp.sum(jnp.where(tgt_row == col, 1.0, 0.0), axis=1, keepdims=True)
        less = jnp.sum(jnp.where((tgt_row < col) & (tgt_row >= first), 1.0, 0.0), axis=1, keepdims=True)
        return hit > 0.5, less

    first = (loop * rows).astype(F32)
    local_row = iota((rows, 1), 0)
    hit, less = count(first, local_row + first)
    pack = jnp.where(jnp.logical_not(hit) & (local_row - less == iota((rows, kept), 1)), 1.0, 0.0).astype(BF16)

    def packed(cols):
        return lax.dot_general(
            pack, gv[:, cols], (((0,), (0,)), ((), ())), preferred_element_type=F32
        ).astype(BF16)

    g_in.wait()
    for k in range(2):
        gb[0, 0, k, c] = packed(pl.ds(pl.multiple_of(h * half + k * part_k, part_k), part_k))
        q_out[k] = packed(pl.ds(pl.multiple_of(other * half + k * part_k, part_k), part_k))
    pl.semaphore_wait(barrier, len(peers))

    def y_copy(pq, d, k, step):
        return remote(
            gb.at[pq, d % NY, k, c], gb.at[pq, (d - step) % NY, k, c],
            y_ss.at[pq, k, 0 if step > 0 else 1, abs(d)], y_rs.at[pq, (d - step) % NY, k], dev(dy=step),
        )

    def b_copy(pq, d, k):
        return remote(
            gb.at[pq, d % NY, k, c], gb.at[pq, d % NY, k, c], b_ss.at[pq, d % NY, k], b_rs.at[pq, d % NY, k], dev(dc=1)
        )

    def b_wait(pq, d, k):
        remote(
            gb.at[pq, d % NY, k, 1 - c], gb.at[pq, d % NY, k, 1 - c],
            b_ss.at[pq, d % NY, k], b_rs.at[pq, d % NY, k], dev(dc=1),
        ).wait_recv()

    def q_copy(k):
        return remote(q_out.at[k], gb.at[1, 0, k, c], p_ss.at[k], p_rs.at[k], dev(dx=2))

    started = []

    def go(copy):
        copy.start()
        started.append(copy)

    go(y_copy(0, 0, 0, 1))
    go(y_copy(0, 0, 1, -1))
    go(q_copy(0))
    go(q_copy(1))
    go(y_copy(0, 0, 1, 1))
    go(y_copy(0, 0, 0, -1))
    go(remote(chol.at[:, far_cols], w_own, p_ss.at[2], p_rs.at[2], dev(dx=2)))
    h_in = remote(chol.at[:, far_cols], w_far, p_ss.at[2], p_rs.at[2], dev(dx=2))
    step_near(0)
    go(b_copy(0, 0, 0))
    go(b_copy(0, 0, 1))

    diag = iota((events, events), 0) == iota((events, events), 1)
    tgt_col = jnp.sum(jnp.where(diag, tgt_row, 0.0), axis=1, keepdims=True)
    pos_row = jnp.sum(jnp.where(tgt_col < tgt_row, 1.0, 0.0), axis=0, keepdims=True)
    src_col = jnp.sum(jnp.where(iota((events, events), 0) == pos_row, src_row, 0.0), axis=1, keepdims=True)
    src_block = jnp.floor((src_col + 0.5) * (1.0 / rows))
    _, src_less = count(src_block * rows, src_col)
    src_kept = src_col - src_block * PER - src_less
    lane = iota((1, 3 * two), 1)
    lane = lane - jnp.where(lane >= two, 1.0 * two, 0.0) - jnp.where(lane >= 2 * two, 1.0 * two, 0.0)
    dist[...] = src_kept - lane
    fix[...] = jnp.zeros_like(fix)
    s_acc[...] = jnp.zeros_like(s_acc)

    parity_here = lax.rem(y + xl, 2)
    far_block = other * 16 + lax.rem(loop, 16)

    def place(pq, d):
        hb = h if pq == 0 else other
        yb = lax.rem(y + (d % NY), NY)
        return hb, yb, 4 * hb + lax.div(yb, 2)

    def x_copy(pq, d, dx, slot):
        to = lax.div(lax.rem(x + dx, NX), 2)
        return remote(
            cs.at[pq, d % NY, to], rx.at[dx - 1, slot], x_ss.at[dx - 1, slot], x_rs.at[dx - 1, slot], dev(dx=dx)
        )

    def compute(pq, d):
        hb, yb, slot = place(pq, d)
        blocks = []
        part = None
        for k in range(2):
            b_wait(pq, d, k)
            a = gb[pq, d % NY, k].reshape(two, part_k)
            blocks.append(a)
            term = dot_t(a, w[:, k * part_k : (k + 1) * part_k])
            part = term if part is None else part + term
        cs[pq, d % NY, 0] = part[:, :vec]
        cs[pq, d % NY, 1] = part[:, vec:]

        @pl.when(parity_here == d % 2)
        def _():
            x_copy(pq, d, 2, slot).start()

        @pl.when(parity_here != d % 2)
        def _():
            x_copy(pq, d, 1, slot).start()
            x_copy(pq, d, 3, slot).start()

        base = ((8 * hb + yb) * two).astype(F32)
        onehot = jnp.where(dist[...] == base, 1.0, 0.0).astype(BF16)
        fix[...] += jnp.dot(onehot, jnp.concatenate(split3(part), axis=0), preferred_element_type=F32)
        d_own = dist[pl.ds(pl.multiple_of(loop * PER, PER), PER), :]
        d_far = dist[pl.ds(pl.multiple_of(far_block * PER, PER), PER), :]
        d_both = jnp.concatenate([d_own, d_far], axis=0)[:, :two]
        onehot_s = jnp.where(d_both == base, 1.0, 0.0).astype(BF16)
        for k in range(2):
            s_acc[k] += jnp.dot(onehot_s, blocks[k], preferred_element_type=F32)

    def z_stage(pq, d):
        _, _, slot = place(pq, d)

        @pl.when(parity_here == d % 2)
        def _():
            for dx in range(1, NX):
                x_copy(pq, d, dx, slot).wait_recv()
            zs[slot] = (cs[pq, d % NY, h] + rx[0, slot]) + (rx[1, slot] + rx[2, slot])
            k = lax.rem(slot - z + NZ, NZ)

            @pl.when(k != 0)
            def _():
                remote(zs.at[slot], rz.at[k], z_ss.at[k], z_rs.at[k], dev(dz=k)).start()

    def take(pq, d, k):
        remote(
            gb.at[pq, d % NY, k, c], gb.at[pq, d % NY, k, c], y_ss.at[pq, k, 0, 0], y_rs.at[pq, d % NY, k], dev(dy=1)
        ).wait_recv()
        up_end, down_end = (4, 3) if k == 0 else (3, 4)
        if d < 0 and -d < up_end:
            go(y_copy(pq, d, k, 1))
        if 0 < d < down_end:
            go(y_copy(pq, d, k, -1))
        go(b_copy(pq, d, k))

    def enter(k):
        q_copy(k).wait_recv()
        go(y_copy(1, 0, k, 1))
        go(y_copy(1, 0, k, -1))
        go(b_copy(1, 0, k))

    take(0, -1, 0)
    take(0, 1, 1)
    enter(0)
    step_near(1)
    take(0, -1, 1)
    take(0, 1, 0)
    enter(1)
    step_near(2)
    take(0, -2, 0)
    take(0, 2, 1)
    take(1, -1, 0)
    take(1, 1, 0)
    step_near(3)
    take(1, -1, 1)
    take(1, 1, 1)
    take(0, -2, 1)
    take(0, 2, 0)
    take(1, -2, 0)
    take(0, 3, 1)
    take(0, -3, 0)
    take(1, 2, 1)
    c_in.wait()
    h_in.wait_recv()
    compute(0, 0)
    compute(1, 0)
    take(1, -2, 1)
    take(1, 2, 0)
    compute(0, -1)
    compute(0, 1)
    compute(1, -1)
    take(1, -3, 0)
    take(0, 3, 0)
    compute(1, 1)
    compute(0, -2)
    z_stage(0, 0)
    z_stage(1, 0)
    take(0, -3, 1)
    take(1, 3, 1)
    compute(0, 2)
    compute(1, -2)
    compute(1, 2)
    take(0, 4, 0)
    take(0, 4, 1)
    compute(0, -3)
    compute(0, 3)
    z_stage(0, -1)
    z_stage(0, 1)
    z_stage(1, -1)
    z_stage(1, 1)
    take(1, -3, 1)
    take(1, 3, 0)
    compute(0, 4)
    z_stage(0, -2)
    z_stage(0, 2)
    take(1, 4, 0)
    take(1, 4, 1)
    compute(1, -3)
    compute(1, 3)
    compute(1, 4)

    full = fix[...]
    for zz in range(NZ):
        for par in range(2):
            r0 = (2 * zz + par) * 16
            fx[par, 0, zz] = full[r0 : r0 + 16, :vec]
            fx[par, 1, zz] = full[r0 : r0 + 16, vec:]

    def fx_copy(dx):
        xx = lax.rem(x + dx, NX)
        return remote(fx.at[lax.rem(xx, 2), lax.div(xx, 2)], rfx.at[dx - 1], fx_ss.at[dx - 1], fx_rs.at[dx - 1], dev(dx=dx))

    for dx in range(1, NX):
        go(fx_copy(dx))
    for k in range(2):
        s_out[:, k * part_k : (k + 1) * part_k] = s_acc[k].astype(BF16)
    s_copy = remote(s_out, s_in, p_ss.at[3], p_rs.at[3], dev(dx=2))
    go(s_copy)
    for d in (-2, 2, -3, 3, 4):
        if abs(d) != 2:
            z_stage(0, d)
        z_stage(1, d)
    for dx in range(1, NX):
        fx_copy(dx).wait_recv()
    fzs[...] = (fx[xl, h] + rfx[0]) + (rfx[1] + rfx[2])

    def fz_copy(k):
        return remote(fzs.at[lax.rem(z + k, NZ)], rfz.at[k], fz_ss.at[k], fz_rs.at[k], dev(dz=k))

    for k in range(1, NZ):
        go(fz_copy(k))

    lane16 = iota((rows, 16), 1)
    put_own = jnp.where(hit & (less == lane16), 1.0, 0.0).astype(BF16)
    put_far = jnp.where(hit & (less + PER == lane16), 1.0, 0.0).astype(BF16)
    keep = jnp.where(jnp.logical_not(hit) & (local_row == iota((rows, rows), 1)), 1.0, 0.0).astype(BF16)
    new_green[:, own_cols] = (
        jnp.dot(keep, gv[:, own_cols], preferred_element_type=F32)
        + jnp.dot(put_own, s_out[...], preferred_element_type=F32)
    ).astype(BF16)
    s_copy.wait_recv()
    new_green[:, far_cols] = (
        jnp.dot(keep, gv[:, far_cols], preferred_element_type=F32)
        + jnp.dot(put_far, s_in[...], preferred_element_type=F32)
    ).astype(BF16)

    wide = 2 * rows
    o_first = (orb * wide).astype(F32)
    o_row = iota((wide, 1), 0)
    in_core = jnp.where(o_row >= rows, 1.0, 0.0)
    o_hit, o_less = count(o_first + in_core * rows, o_row + o_first)
    o_from = jnp.where(o_hit, two + in_core * PER + o_less, o_row - in_core * PER - o_less)
    order = jnp.where(o_from == iota((wide, wide), 1), 1.0, 0.0).astype(BF16)
    main = zs[z]
    tail = fzs[z]
    for k in range(1, NZ):
        remote(zs.at[0], rz.at[k], z_ss.at[k], z_rs.at[k], dev(dz=k)).wait_recv()
        main = main + rz[k]
    for k in range(1, NZ):
        fz_copy(k).wait_recv()
        tail = tail + rfz[k]
    bias[...] = pick_rows(order, jnp.concatenate([main, tail], axis=0))

    for copy in started:
        copy.wait_send()
    for dx in range(1, NX):
        for slot in range(NZ):
            remote(cs.at[0, 0, 0], rx.at[dx - 1, slot], x_ss.at[dx - 1, slot], x_rs.at[dx - 1, slot], dev(dx=dx)).wait_send()
    for k in range(1, NZ):
        remote(zs.at[0], rz.at[k], z_ss.at[k], z_rs.at[k], dev(dz=k)).wait_send()


def local(cholesky, green_half, partners):
    rows, depth = green_half.shape
    vec = cholesky.shape[0]
    half, two = depth // 2, 2 * (rows - PER)
    kept, part_k = rows - PER, half // 2
    dma = pltpu.SemaphoreType.DMA
    vmem = pl.BlockSpec(memory_space=pltpu.VMEM)
    hbm = pl.BlockSpec(memory_space=pl.ANY)
    return pl.pallas_call(
        kernel,
        out_shape=(
            jax.ShapeDtypeStruct((rows, depth), BF16),
            jax.ShapeDtypeStruct((2 * rows, vec), F32),
        ),
        in_specs=[hbm] * 3,
        out_specs=(vmem, vmem),
        scratch_shapes=[
            pltpu.VMEM((rows, depth), BF16),
            pltpu.VMEM((2, 256), jnp.int32),
            pltpu.VMEM((2, NY, 2, 2, kept, part_k), BF16),
            pltpu.VMEM((2 * vec, half), BF16),
            pltpu.VMEM((2, NY, 2, two, vec), F32),
            pltpu.VMEM((3, NZ, two, vec), F32),
            pltpu.VMEM((NZ, two, vec), F32),
            pltpu.VMEM((NZ, two, vec), F32),
            pltpu.VMEM((256, 2 * vec), F32),
            pltpu.VMEM((2, 2, NZ, 16, vec), F32),
            pltpu.VMEM((3, NZ, 16, vec), F32),
            pltpu.VMEM((NZ, 16, vec), F32),
            pltpu.VMEM((NZ, 16, vec), F32),
            pltpu.VMEM((2, 16, part_k), F32),
            pltpu.VMEM((16, half), BF16),
            pltpu.VMEM((16, half), BF16),
            pltpu.VMEM((2, kept, part_k), BF16),
            pltpu.VMEM((256, 3 * two), F32),
            dma((3,)),
            dma((2, 2, 2, 4)), dma((2, NY, 2)), dma((2, NY, 2)), dma((2, NY, 2)), dma((4,)), dma((4,)),
            dma((3, NZ)), dma((3, NZ)), dma((NZ,)), dma((NZ,)), dma((3,)), dma((3,)), dma((NZ,)), dma((NZ,)),
            pltpu.SemaphoreType.REGULAR((3,)),
        ],
        compiler_params=pltpu.CompilerParams(
            collective_id=0, has_side_effects=True, vmem_limit_bytes=60 * 1024 * 1024
        ),
    )(cholesky, green_half, partners.T)


def solution(mesh):
    return jax.shard_map(
        local,
        mesh=mesh,
        in_specs=(P("loop", "orb"), P("loop", "orb"), P()),
        out_specs=(P("loop", "orb"), P("orb", "loop")),
        check_vma=False,
    )
```

```python
import jax
import jax.numpy as jnp
from jax import lax
from jax.experimental import pallas as pl
from jax.experimental.pallas import tpu as pltpu
from jax.sharding import PartitionSpec as P

MESH = pl.DeviceIdType.MESH
NY, NZ, NX = 8, 8, 4
PER = 8
F32, BF16 = jnp.float32, jnp.bfloat16


def dot_t(a, b):
    return lax.dot_general(a, b, (((1,), (1,)), ((), ())), preferred_element_type=F32)


def split3(v):
    hi = v.astype(BF16)
    rest = v - hi.astype(F32)
    mid = rest.astype(BF16)
    lo = (rest - mid.astype(F32)).astype(BF16)
    return hi, mid, lo


def pick_rows(onehot, v):
    hi, mid, lo = split3(v)
    return (
        jnp.dot(onehot, hi, preferred_element_type=F32)
        + jnp.dot(onehot, mid, preferred_element_type=F32)
    ) + jnp.dot(onehot, lo, preferred_element_type=F32)


def iota(shape, dim):
    return lax.broadcasted_iota(jnp.int32, shape, dim).astype(F32)


def kernel(
    chol, green, prow, new_green, bias,
    gv, pv, ga, gb, w, cs, rx, zs, rz, fs, rfs, fss, rfsz, fd, rfd, fdd, rfdx, ng, s_out, s_in, qa_out, qb_out, c_src, rel, in_s,
    y_ss, y_rs, b_ss, b_rs, p_ss, p_rs, x_ss, x_rs, z_ss, z_rs, e_ss, e_rs, near,
):
    rows = green.shape[0]
    vec = chol.shape[0]
    half = green.shape[1] // 2
    part_k = half // 2
    kept = rows - 2 * PER
    two = 2 * kept
    events = prow.shape[1]
    loop, orb = lax.axis_index("loop"), lax.axis_index("orb")
    h, y, c = lax.div(loop, 16), lax.rem(lax.div(loop, 2), NY), lax.rem(loop, 2)
    z, xl = lax.div(orb, 2), lax.rem(orb, 2)
    x = 2 * h + xl
    other = 1 - h

    def dev(dx=0, dy=0, dz=0, dc=0):
        xx = lax.rem(x + dx, NX)
        yy = lax.rem(y + dy + NY, NY)
        zz = lax.rem(z + dz + NZ, NZ)
        cc = lax.rem(c + dc, 2)
        return (lax.div(xx, 2) * 16 + yy * 2 + cc, zz * 2 + lax.rem(xx, 2))

    def remote(src, dst, ss, rs, to):
        return pltpu.make_async_remote_copy(
            src_ref=src, dst_ref=dst, send_sem=ss, recv_sem=rs, device_id=to, device_id_type=MESH
        )

    def signal(sem, to):
        pl.semaphore_signal(sem, inc=1, device_id=to, device_id_type=MESH)

    own_cols = pl.ds(pl.multiple_of(h * half, half), half)
    far_cols = pl.ds(pl.multiple_of(other * half, half), half)
    w_own = w.at[pl.ds(pl.multiple_of(h * vec, vec), vec)]
    w_far = w.at[pl.ds(pl.multiple_of(other * vec, vec), vec)]
    p_in = pltpu.make_async_copy(prow, pv, in_s.at[0])
    g_in = pltpu.make_async_copy(green, gv, in_s.at[1])
    c_in = pltpu.make_async_copy(chol.at[:, own_cols], w_own, in_s.at[2])
    p_in.start()
    g_in.start()
    c_in.start()

    barrier = pltpu.get_barrier_semaphore()
    peers = [dev(dy=1), dev(dy=-1), dev(dc=1), dev(dz=1), dev(dz=-1)] + [dev(dx=k) for k in range(1, NX)]
    for peer in peers:
        signal(barrier, peer)

    def step_near(r):
        if r > 0:
            pl.semaphore_wait(near.at[r - 1], 2)
        if r < 3:
            signal(near.at[r], dev(dz=1))
            signal(near.at[r], dev(dz=-1))

    p_in.wait()
    src_row, tgt_row = pv[0:1, :].astype(F32), pv[1:2, :].astype(F32)

    def count(row, first, col):
        hit = jnp.sum(jnp.where(row == col, 1.0, 0.0), axis=1, keepdims=True)
        less = jnp.sum(jnp.where((row < col) & (row >= first), 1.0, 0.0), axis=1, keepdims=True)
        return hit, less

    first = (loop * rows).astype(F32)
    local_row = iota((rows, 1), 0)
    hit_t, less = count(tgt_row, first, local_row + first)
    hit_s, less_s = count(src_row, first, local_row + first)
    hit = hit_t > 0.5
    pack_a = jnp.where((hit_s > 0.5) & (less_s == iota((rows, PER), 1)), 1.0, 0.0).astype(BF16)
    pack_b = jnp.where(
        (hit_s + hit_t < 0.5) & (local_row - less - less_s == iota((rows, kept), 1)), 1.0, 0.0
    ).astype(BF16)

    def packed(pack, which, k):
        cols = pl.ds(pl.multiple_of(which * half + k * part_k, part_k), part_k)
        return lax.dot_general(pack, gv[:, cols], (((0,), (0,)), ((), ())), preferred_element_type=F32)

    def chunk(pq, d, kind, core):
        return ga.at[pq, d % NY, core] if kind == 2 else gb.at[pq, d % NY, kind, core]

    def y_copy(pq, d, kind, step):
        return remote(
            chunk(pq, d, kind, c), chunk(pq, d - step, kind, c),
            y_ss.at[pq, kind, 0 if step > 0 else 1, abs(d)], y_rs.at[pq, (d - step) % NY, kind], dev(dy=step),
        )

    def b_copy(pq, d, kind):
        return remote(
            chunk(pq, d, kind, c), chunk(pq, d, kind, c), b_ss.at[pq, d % NY, kind], b_rs.at[pq, d % NY, kind], dev(dc=1)
        )

    def b_wait(pq, d, kind):
        remote(
            chunk(pq, d, kind, 1 - c), chunk(pq, d, kind, 1 - c),
            b_ss.at[pq, d % NY, kind], b_rs.at[pq, d % NY, kind], dev(dc=1),
        ).wait_recv()

    def q_copy(kind):
        src = qa_out if kind == 2 else qb_out.at[kind]
        return remote(src, chunk(1, 0, kind, c), p_ss.at[kind], p_rs.at[kind], dev(dx=2))

    started = []

    def go(copy):
        copy.start()
        started.append(copy)

    g_in.wait()
    ga[0, 0, c] = jnp.concatenate([packed(pack_a, h, k) for k in range(2)], axis=0).astype(BF16)
    gb[0, 0, 0, c] = packed(pack_b, h, 0).astype(BF16)
    pl.semaphore_wait(barrier, len(peers))
    go(y_copy(0, 0, 2, 1))
    go(y_copy(0, 0, 2, -1))
    go(y_copy(0, 0, 0, 1))
    gb[0, 0, 1, c] = packed(pack_b, h, 1).astype(BF16)
    go(y_copy(0, 0, 1, -1))
    qa_out[...] = jnp.concatenate([packed(pack_a, other, k) for k in range(2)], axis=0).astype(BF16)
    go(q_copy(2))
    qb_out[0] = packed(pack_b, other, 0).astype(BF16)
    go(q_copy(0))
    go(y_copy(0, 0, 1, 1))
    go(y_copy(0, 0, 0, -1))
    qb_out[1] = packed(pack_b, other, 1).astype(BF16)
    go(q_copy(1))
    go(remote(chol.at[:, far_cols], w_own, p_ss.at[3], p_rs.at[3], dev(dx=2)))
    h_in = remote(chol.at[:, far_cols], w_far, p_ss.at[3], p_rs.at[3], dev(dx=2))
    step_near(0)
    for kind in (2, 0, 1):
        go(b_copy(0, 0, kind))

    diag = iota((events, events), 0) == iota((events, events), 1)
    tgt_col = jnp.sum(jnp.where(diag, tgt_row, 0.0), axis=1, keepdims=True)
    pos_row = jnp.sum(jnp.where(tgt_col < tgt_row, 1.0, 0.0), axis=0, keepdims=True)
    src_col = jnp.sum(jnp.where(iota((events, events), 0) == pos_row, src_row, 0.0), axis=1, keepdims=True)
    src_block = jnp.floor((src_col + 0.5) * (1.0 / rows))
    _, rank = count(src_row, src_block * rows, src_col)
    src_h = jnp.floor((src_block + 0.5) * (1.0 / 16))
    src_y = jnp.floor((src_block - 16.0 * src_h + 0.5) * 0.5)
    src_c = src_block - 16.0 * src_h - 2.0 * src_y
    src_d = src_y - y.astype(F32)
    src_d = src_d + jnp.where(src_d < 0.0, 1.0 * NY, 0.0)
    src_at = 2.0 * (NY * jnp.abs(src_h - h.astype(F32)) + src_d) + src_c
    rel[...] = jnp.broadcast_to(src_at * (2 * PER) + rank, rel.shape)

    parity_here = lax.rem(y + xl, 2)
    far_block = other * 16 + lax.rem(loop, 16)

    def place(pq, d):
        hb = h if pq == 0 else other
        yb = lax.rem(y + (d % NY), NY)
        return hb, yb, 4 * hb + lax.div(yb, 2)

    def x_copy(pq, d, dx, slot):
        to = lax.div(lax.rem(x + dx, NX), 2)
        return remote(
            cs.at[pq, d % NY, to], rx.at[dx - 1, slot], x_ss.at[dx - 1, slot], x_rs.at[dx - 1, slot], dev(dx=dx)
        )

    def compute(pq, d):
        _, _, slot = place(pq, d)
        part = None
        for k in range(2):
            b_wait(pq, d, k)
            term = dot_t(gb[pq, d % NY, k].reshape(two, part_k), w[:, k * part_k : (k + 1) * part_k])
            part = term if part is None else part + term
        cs[pq, d % NY, 0] = part[:, :vec]
        cs[pq, d % NY, 1] = part[:, vec:]

        @pl.when(parity_here == d % 2)
        def _():
            x_copy(pq, d, 2, slot).start()

        @pl.when(parity_here != d % 2)
        def _():
            x_copy(pq, d, 1, slot).start()
            x_copy(pq, d, 3, slot).start()

    def z_stage(pq, d):
        _, _, slot = place(pq, d)

        @pl.when(parity_here == d % 2)
        def _():
            for dx in range(1, NX):
                x_copy(pq, d, dx, slot).wait_recv()
            zs[slot] = (cs[pq, d % NY, h] + rx[0, slot]) + (rx[1, slot] + rx[2, slot])
            k = lax.rem(slot - z + NZ, NZ)

            @pl.when(k != 0)
            def _():
                remote(zs.at[slot], rz.at[k], z_ss.at[k], z_rs.at[k], dev(dz=k)).start()

    def take(pq, d, kind):
        remote(
            chunk(pq, d, kind, c), chunk(pq, d, kind, c), y_ss.at[pq, kind, 0, 0], y_rs.at[pq, d % NY, kind], dev(dy=1)
        ).wait_recv()
        long_up = kind == 0 or (kind == 2 and pq == 0)
        up_end, down_end = (4, 3) if long_up else (3, 4)
        if d < 0 and -d < up_end:
            go(y_copy(pq, d, kind, 1))
        if 0 < d < down_end:
            go(y_copy(pq, d, kind, -1))
        go(b_copy(pq, d, kind))

    def enter(kind):
        q_copy(kind).wait_recv()
        go(y_copy(1, 0, kind, 1))
        go(y_copy(1, 0, kind, -1))
        go(b_copy(1, 0, kind))

    def source_parts():
        both = 2 * PER
        for pq in range(2):
            for d in range(NY):
                b_wait(pq, d, 2)
        a = ga[...].reshape(2 * NY * 2 * both, part_k)
        t = [dot_t(a, w[:, k * part_k : (k + 1) * part_k]).reshape(4 * NY, both, 2 * vec) for k in range(2)]
        c_src[...] = (t[0][:, :PER] + t[1][:, PER:]).reshape(4 * NY * PER, 2 * vec)

    def fs_x(dx):
        xx = lax.rem(x + dx, NX)
        return remote(fs.at[lax.rem(xx, 2), lax.div(xx, 2)], rfs.at[dx - 1], e_ss.at[0, dx], e_rs.at[0, dx], dev(dx=dx))

    def fs_z(k):
        return remote(fss.at[lax.rem(z + k, NZ)], rfsz.at[k], e_ss.at[1, k], e_rs.at[1, k], dev(dz=k))

    def fd_z(k):
        return remote(fd.at[lax.rem(z + k, NZ)], rfd.at[k], e_ss.at[2, k], e_rs.at[2, k], dev(dz=k))

    def fd_x(dx):
        xx = lax.rem(x + dx, NX)
        return remote(fdd.at[lax.rem(xx, 2), lax.div(xx, 2)], rfdx.at[dx - 1], e_ss.at[3, dx], e_rs.at[3, dx], dev(dx=dx))

    def source_send():
        sums = c_src[...]
        both = 2 * PER
        for pq in range(2):
            for d in range(NY):
                _, yb, slot = place(pq, d)
                r0 = (pq * NY + d) * both
                for g in range(2):
                    fs[lax.rem(yb, 2), g, slot] = sums[r0 : r0 + both, g * vec : (g + 1) * vec]
        for dx in range(1, NX):
            go(fs_x(dx))
        block = jnp.floor((rel[:, 0:1] + 0.5) * (1.0 / (2 * PER)))
        at = rel[:, 0:1] - PER * block
        picked = pick_rows(jnp.where(at == iota((events, events), 1), 1.0, 0.0).astype(BF16), sums)
        for zz in range(NZ):
            for par in range(2):
                r0 = (2 * zz + par) * both
                for g in range(2):
                    fd[zz, par, g] = picked[r0 : r0 + both, g * vec : (g + 1) * vec]
        for k in range(1, NZ):
            go(fd_z(k))

    s_copy = remote(s_out, s_in, p_ss.at[4], p_rs.at[4], dev(dx=2))

    def rows_send():
        here = rel[pl.ds(pl.multiple_of(loop * PER, PER), PER), :]
        there = rel[pl.ds(pl.multiple_of(far_block * PER, PER), PER), :]
        at = jnp.concatenate([here, there], axis=0)[:, 0:1]
        a = ga[...].reshape(8 * NY * PER, part_k)
        for k in range(2):
            onehot = jnp.where(at + k * PER == iota((2 * PER, 8 * NY * PER), 1), 1.0, 0.0).astype(BF16)
            s_out[:, k * part_k : (k + 1) * part_k] = jnp.dot(onehot, a, preferred_element_type=F32).astype(BF16)
        go(s_copy)

    g_out = pltpu.make_async_copy(ng, new_green, in_s.at[3])

    def rows_out():
        s_copy.wait_recv()
        lane16 = iota((rows, 2 * PER), 1)
        put_own = jnp.where(hit & (less == lane16), 1.0, 0.0).astype(BF16)
        put_far = jnp.where(hit & (less + PER == lane16), 1.0, 0.0).astype(BF16)
        keep = jnp.where(jnp.logical_not(hit) & (local_row == iota((rows, rows), 1)), 1.0, 0.0).astype(BF16)
        for cols, put, got in ((own_cols, put_own, s_out), (far_cols, put_far, s_in)):
            ng[:, cols] = (
                jnp.dot(keep, gv[:, cols], preferred_element_type=F32)
                + jnp.dot(put, got[...], preferred_element_type=F32)
            ).astype(BF16)
        g_out.start()

    def sources_on():
        for dx in range(1, NX):
            fs_x(dx).wait_recv()
        fss[...] = (fs[xl, h] + rfs[0]) + (rfs[1] + rfs[2])
        for k in range(1, NZ):
            go(fs_z(k))

    def destinations_on():
        total = fd[z]
        for k in range(1, NZ):
            fd_z(k).wait_recv()
            total = total + rfd[k]
        fdd[...] = total
        for dx in range(1, NX):
            go(fd_x(dx))

    def takes(*items):
        for item in items:
            take(*item)

    takes((0, -1, 2), (0, 1, 2))
    enter(2)
    takes((0, -1, 0), (0, 1, 1))
    step_near(1)
    enter(0)
    takes((0, -1, 1), (0, 1, 0), (0, -2, 2), (0, 2, 2))
    enter(1)
    step_near(2)
    takes((1, -1, 2), (1, 1, 2), (0, -2, 0), (0, 2, 1), (1, -1, 0), (1, 1, 0))
    step_near(3)
    takes((0, -3, 2), (0, 3, 2), (1, -2, 2), (1, 2, 2), (1, -1, 1), (1, 1, 1), (0, -2, 1), (0, 2, 0))
    c_in.wait()
    h_in.wait_recv()
    compute(0, 0)
    takes((0, 4, 2), (0, 3, 1))
    compute(1, 0)
    takes((1, -3, 2), (1, 3, 2))
    compute(0, -1)
    takes((1, -2, 0), (1, 2, 1))
    compute(0, 1)
    takes((0, -3, 0), (1, 2, 0))
    compute(1, -1)
    takes((1, 4, 2), (1, -2, 1), (0, 3, 0))
    compute(1, 1)
    source_parts()
    source_send()
    takes((0, -3, 1), (1, -3, 0), (1, 3, 1))
    for d in (-2, 2):
        compute(0, d)
    for d in (-2, 2):
        compute(1, d)
    takes((0, 4, 0), (0, 4, 1))
    for d in (-3, 3):
        compute(0, d)
    compute(0, 4)
    takes((1, -3, 1), (1, 3, 0))
    rows_send()
    for d in (0, -1, 1):
        z_stage(0, d)
        z_stage(1, d)
    for d in (-3, 3):
        compute(1, d)
    takes((1, 4, 0), (1, 4, 1))
    compute(1, 4)
    sources_on()
    for d in (-2, 2, -3, 3, 4):
        z_stage(0, d)
        z_stage(1, d)
    destinations_on()
    rows_out()

    wide = 2 * rows
    o_first = (orb * wide).astype(F32)
    o_row = iota((wide, 1), 0)
    in_core = jnp.where(o_row >= rows, 1.0, 0.0)
    o_base, o_abs = o_first + in_core * rows, o_row + o_first
    hit_o, t_less = count(tgt_row, o_base, o_abs)
    hit_i, s_less = count(src_row, o_base, o_abs)
    o_from = o_row - in_core * (rows - kept) - t_less - s_less
    o_from = jnp.where(hit_i > 0.5, two + in_core * PER + s_less, o_from)
    o_from = jnp.where(hit_o > 0.5, two + (2 + in_core) * PER + t_less, o_from)
    order = jnp.where(o_from == iota((wide, wide), 1), 1.0, 0.0).astype(BF16)
    main, from_s, from_d = zs[z], fss[z], fdd[xl, h]
    for dx in range(1, NX):
        fd_x(dx).wait_recv()
        from_d = from_d + rfdx[dx - 1]
    for k in range(1, NZ):
        fs_z(k).wait_recv()
        from_s = from_s + rfsz[k]
    for k in range(1, NZ):
        remote(zs.at[0], rz.at[k], z_ss.at[k], z_rs.at[k], dev(dz=k)).wait_recv()
        main = main + rz[k]
    bias[...] = pick_rows(order, jnp.concatenate([main, from_s, from_d], axis=0))

    g_out.wait()
    for copy in started:
        copy.wait_send()
    for dx in range(1, NX):
        for slot in range(NZ):
            remote(cs.at[0, 0, 0], rx.at[dx - 1, slot], x_ss.at[dx - 1, slot], x_rs.at[dx - 1, slot], dev(dx=dx)).wait_send()
    for k in range(1, NZ):
        remote(zs.at[0], rz.at[k], z_ss.at[k], z_rs.at[k], dev(dz=k)).wait_send()


def local(cholesky, green_half, partners):
    rows, depth = green_half.shape
    vec = cholesky.shape[0]
    half, kept = depth // 2, rows - 2 * PER
    two, part_k, both = 2 * kept, half // 2, 2 * PER
    dma = pltpu.SemaphoreType.DMA
    vmem = pl.BlockSpec(memory_space=pltpu.VMEM)
    hbm = pl.BlockSpec(memory_space=pl.ANY)
    return pl.pallas_call(
        kernel,
        out_shape=(
            jax.ShapeDtypeStruct((rows, depth), BF16),
            jax.ShapeDtypeStruct((2 * rows, vec), F32),
        ),
        in_specs=[hbm] * 3,
        out_specs=(hbm, vmem),
        scratch_shapes=[
            pltpu.VMEM((rows, depth), BF16),
            pltpu.VMEM((2, 256), jnp.int32),
            pltpu.VMEM((2, NY, 2, both, part_k), BF16),
            pltpu.VMEM((2, NY, 2, 2, kept, part_k), BF16),
            pltpu.VMEM((2 * vec, half), BF16),
            pltpu.VMEM((2, NY, 2, two, vec), F32),
            pltpu.VMEM((3, NZ, two, vec), F32),
            pltpu.VMEM((NZ, two, vec), F32),
            pltpu.VMEM((NZ, two, vec), F32),
            pltpu.VMEM((2, 2, NZ, both, vec), F32),
            pltpu.VMEM((3, NZ, both, vec), F32),
            pltpu.VMEM((NZ, both, vec), F32),
            pltpu.VMEM((NZ, both, vec), F32),
            pltpu.VMEM((NZ, 2, 2, both, vec), F32),
            pltpu.VMEM((NZ, 2, 2, both, vec), F32),
            pltpu.VMEM((2, 2, both, vec), F32),
            pltpu.VMEM((3, both, vec), F32),
            pltpu.VMEM((rows, depth), BF16),
            pltpu.VMEM((both, half), BF16),
            pltpu.VMEM((both, half), BF16),
            pltpu.VMEM((both, part_k), BF16),
            pltpu.VMEM((2, kept, part_k), BF16),
            pltpu.VMEM((256, 2 * vec), F32),
            pltpu.VMEM((256, 128), F32),
            dma((4,)),
            dma((2, 3, 2, 4)), dma((2, NY, 3)), dma((2, NY, 3)), dma((2, NY, 3)), dma((5,)), dma((5,)),
            dma((3, NZ)), dma((3, NZ)), dma((NZ,)), dma((NZ,)), dma((4, NZ)), dma((4, NZ)),
            pltpu.SemaphoreType.REGULAR((3,)),
        ],
        compiler_params=pltpu.CompilerParams(
            collective_id=0, has_side_effects=True, vmem_limit_bytes=60 * 1024 * 1024
        ),
    )(cholesky, green_half, partners.T)


def solution(mesh):
    return jax.shard_map(
        local,
        mesh=mesh,
        in_specs=(P("loop", "orb"), P("loop", "orb"), P()),
        out_specs=(P("loop", "orb"), P("orb", "loop")),
        check_vma=False,
    )
```

```python
import jax
import jax.numpy as jnp
from jax import lax
from jax.experimental import pallas as pl
from jax.experimental.pallas import tpu as pltpu
from jax.sharding import PartitionSpec as P

MESH = pl.DeviceIdType.MESH
NY, NZ, NX = 8, 8, 4
PER = 8
F32, BF16 = jnp.float32, jnp.bfloat16


def dot_t(a, b):
    return lax.dot_general(a, b, (((1,), (1,)), ((), ())), preferred_element_type=F32)


def split3(v):
    hi = v.astype(BF16)
    rest = v - hi.astype(F32)
    mid = rest.astype(BF16)
    lo = (rest - mid.astype(F32)).astype(BF16)
    return hi, mid, lo


def pick_rows(onehot, v):
    hi, mid, lo = split3(v)
    return (
        jnp.dot(onehot, hi, preferred_element_type=F32)
        + jnp.dot(onehot, mid, preferred_element_type=F32)
    ) + jnp.dot(onehot, lo, preferred_element_type=F32)


def iota(shape, dim):
    return lax.broadcasted_iota(jnp.int32, shape, dim).astype(F32)


def kernel(
    chol, green, prow, new_green, bias,
    gv, pv, ga, gb, w, cs, rx, zs, rz, fs, rfs, fss, rfsz, fd, rfd, fdd, rfdx, ng, s_out, s_in, qa_out, qb_out, c_src, rel, in_s,
    y_ss, y_rs, b_ss, b_rs, p_ss, p_rs, x_ss, x_rs, z_ss, z_rs, e_ss, e_rs, near,
):
    rows = green.shape[0]
    vec = chol.shape[0]
    half = green.shape[1] // 2
    part_k = half // 2
    kept = rows - 2 * PER
    two = 2 * kept
    events = prow.shape[1]
    loop, orb = lax.axis_index("loop"), lax.axis_index("orb")
    h, y, c = lax.div(loop, 16), lax.rem(lax.div(loop, 2), NY), lax.rem(loop, 2)
    z, xl = lax.div(orb, 2), lax.rem(orb, 2)
    x = 2 * h + xl
    other = 1 - h

    def dev(dx=0, dy=0, dz=0, dc=0):
        xx = lax.rem(x + dx, NX)
        yy = lax.rem(y + dy + NY, NY)
        zz = lax.rem(z + dz + NZ, NZ)
        cc = lax.rem(c + dc, 2)
        return (lax.div(xx, 2) * 16 + yy * 2 + cc, zz * 2 + lax.rem(xx, 2))

    def remote(src, dst, ss, rs, to):
        return pltpu.make_async_remote_copy(
            src_ref=src, dst_ref=dst, send_sem=ss, recv_sem=rs, device_id=to, device_id_type=MESH
        )

    def signal(sem, to):
        pl.semaphore_signal(sem, inc=1, device_id=to, device_id_type=MESH)

    own_cols = pl.ds(pl.multiple_of(h * half, half), half)
    far_cols = pl.ds(pl.multiple_of(other * half, half), half)
    w_own = w.at[pl.ds(pl.multiple_of(h * vec, vec), vec)]
    w_far = w.at[pl.ds(pl.multiple_of(other * vec, vec), vec)]
    p_in = pltpu.make_async_copy(prow, pv, in_s.at[0])
    g_in = pltpu.make_async_copy(green, gv, in_s.at[1])
    c_in = pltpu.make_async_copy(chol.at[:, own_cols], w_own, in_s.at[2])
    p_in.start()
    g_in.start()
    c_in.start()

    barrier = pltpu.get_barrier_semaphore()
    peers = [dev(dy=1), dev(dy=-1), dev(dc=1), dev(dz=1), dev(dz=-1)] + [dev(dx=k) for k in range(1, NX)]
    for peer in peers:
        signal(barrier, peer)

    def step_near(r):
        if r > 0:
            pl.semaphore_wait(near.at[r - 1], 2)
        if r < 3:
            signal(near.at[r], dev(dz=1))
            signal(near.at[r], dev(dz=-1))

    p_in.wait()
    src_row, tgt_row = pv[0:1, :].astype(F32), pv[1:2, :].astype(F32)

    def count(row, first, col):
        hit = jnp.sum(jnp.where(row == col, 1.0, 0.0), axis=1, keepdims=True)
        less = jnp.sum(jnp.where((row < col) & (row >= first), 1.0, 0.0), axis=1, keepdims=True)
        return hit, less

    first = (loop * rows).astype(F32)
    local_row = iota((rows, 1), 0)
    hit_t, less = count(tgt_row, first, local_row + first)
    hit_s, less_s = count(src_row, first, local_row + first)
    hit = hit_t > 0.5
    pack_a = jnp.where((hit_s > 0.5) & (less_s == iota((rows, PER), 1)), 1.0, 0.0).astype(BF16)
    pack_b = jnp.where(
        (hit_s + hit_t < 0.5) & (local_row - less - less_s == iota((rows, kept), 1)), 1.0, 0.0
    ).astype(BF16)

    def packed(pack, which, k):
        cols = pl.ds(pl.multiple_of(which * half + k * part_k, part_k), part_k)
        return lax.dot_general(pack, gv[:, cols], (((0,), (0,)), ((), ())), preferred_element_type=F32)

    def chunk(pq, d, kind, core):
        return ga.at[pq, d % NY, core] if kind == 2 else gb.at[pq, d % NY, kind, core]

    def y_copy(pq, d, kind, step):
        return remote(
            chunk(pq, d, kind, c), chunk(pq, d - step, kind, c),
            y_ss.at[kind], y_rs.at[pq, (d - step) % NY, kind], dev(dy=step),
        )

    def b_copy(pq, d, kind):
        return remote(
            chunk(pq, d, kind, c), chunk(pq, d, kind, c),
            b_ss.at[kind // 2], b_rs.at[2 * NY if kind == 2 else pq * NY + d % NY], dev(dc=1),
        )

    def all_of(ref, ss, rs):
        return remote(ref, ref, ss, rs, dev(dc=1))

    def q_copy(kind):
        src = qa_out if kind == 2 else qb_out.at[kind]
        return remote(src, chunk(1, 0, kind, c), p_ss.at[kind], p_rs.at[kind], dev(dx=2))

    started = []

    def go(copy):
        copy.start()
        started.append(copy)

    g_in.wait()
    ga[0, 0, c] = jnp.concatenate([packed(pack_a, h, k) for k in range(2)], axis=0).astype(BF16)
    gb[0, 0, 0, c] = packed(pack_b, h, 0).astype(BF16)
    pl.semaphore_wait(barrier, len(peers))
    y_copy(0, 0, 2, 1).start()
    y_copy(0, 0, 2, -1).start()
    y_copy(0, 0, 0, 1).start()
    gb[0, 0, 1, c] = packed(pack_b, h, 1).astype(BF16)
    y_copy(0, 0, 1, -1).start()
    qa_out[...] = jnp.concatenate([packed(pack_a, other, k) for k in range(2)], axis=0).astype(BF16)
    go(q_copy(2))
    qb_out[0] = packed(pack_b, other, 0).astype(BF16)
    go(q_copy(0))
    y_copy(0, 0, 1, 1).start()
    y_copy(0, 0, 0, -1).start()
    qb_out[1] = packed(pack_b, other, 1).astype(BF16)
    go(q_copy(1))
    go(remote(chol.at[:, far_cols], w_own, p_ss.at[3], p_rs.at[3], dev(dx=2)))
    h_in = remote(chol.at[:, far_cols], w_far, p_ss.at[3], p_rs.at[3], dev(dx=2))
    step_near(0)
    for kind in (2, 0, 1):
        b_copy(0, 0, kind).start()

    diag = iota((events, events), 0) == iota((events, events), 1)
    tgt_col = jnp.sum(jnp.where(diag, tgt_row, 0.0), axis=1, keepdims=True)
    pos_row = jnp.sum(jnp.where(tgt_col < tgt_row, 1.0, 0.0), axis=0, keepdims=True)
    src_col = jnp.sum(jnp.where(iota((events, events), 0) == pos_row, src_row, 0.0), axis=1, keepdims=True)
    src_block = jnp.floor((src_col + 0.5) * (1.0 / rows))
    _, rank = count(src_row, src_block * rows, src_col)
    src_h = jnp.floor((src_block + 0.5) * (1.0 / 16))
    src_y = jnp.floor((src_block - 16.0 * src_h + 0.5) * 0.5)
    src_c = src_block - 16.0 * src_h - 2.0 * src_y
    src_d = src_y - y.astype(F32)
    src_d = src_d + jnp.where(src_d < 0.0, 1.0 * NY, 0.0)
    src_at = 2.0 * (NY * jnp.abs(src_h - h.astype(F32)) + src_d) + src_c
    rel[...] = jnp.broadcast_to(src_at * (2 * PER) + rank, rel.shape)

    parity_here = lax.rem(y + xl, 2)
    far_block = other * 16 + lax.rem(loop, 16)

    def place(pq, d):
        hb = h if pq == 0 else other
        yb = lax.rem(y + (d % NY), NY)
        return hb, yb, 4 * hb + lax.div(yb, 2)

    def x_copy(pq, d, dx, slot):
        to = lax.div(lax.rem(x + dx, NX), 2)
        return remote(
            cs.at[pq, d % NY, to], rx.at[dx - 1, slot], x_ss.at[0], x_rs.at[slot], dev(dx=dx)
        )

    def compute(pq, d):
        _, _, slot = place(pq, d)
        part = None
        all_of(gb.at[pq, d % NY, :, 1 - c], b_ss.at[0], b_rs.at[pq * NY + d % NY]).wait_recv()
        for k in range(2):
            term = dot_t(gb[pq, d % NY, k].reshape(two, part_k), w[:, k * part_k : (k + 1) * part_k])
            part = term if part is None else part + term
        cs[pq, d % NY, 0] = part[:, :vec]
        cs[pq, d % NY, 1] = part[:, vec:]

        @pl.when(parity_here == d % 2)
        def _():
            x_copy(pq, d, 2, slot).start()

        @pl.when(parity_here != d % 2)
        def _():
            x_copy(pq, d, 1, slot).start()
            x_copy(pq, d, 3, slot).start()

    def z_stage(pq, d):
        _, _, slot = place(pq, d)

        @pl.when(parity_here == d % 2)
        def _():
            all_of(rx.at[:, slot], x_ss.at[0], x_rs.at[slot]).wait_recv()
            zs[slot] = (cs[pq, d % NY, h] + rx[0, slot]) + (rx[1, slot] + rx[2, slot])
            k = lax.rem(slot - z + NZ, NZ)

            @pl.when(k != 0)
            def _():
                remote(zs.at[slot], rz.at[k], z_ss.at[0], z_rs.at[0], dev(dz=k)).start()

    def take(pq, d, kind):
        remote(
            chunk(pq, d, kind, c), chunk(pq, d, kind, c), y_ss.at[kind], y_rs.at[pq, d % NY, kind], dev(dy=1)
        ).wait_recv()
        long_up = kind == 0 or (kind == 2 and pq == 0)
        up_end, down_end = (4, 3) if long_up else (3, 4)
        if d < 0 and -d < up_end:
            y_copy(pq, d, kind, 1).start()
        if 0 < d < down_end:
            y_copy(pq, d, kind, -1).start()
        b_copy(pq, d, kind).start()

    def enter(kind):
        q_copy(kind).wait_recv()
        y_copy(1, 0, kind, 1).start()
        y_copy(1, 0, kind, -1).start()
        b_copy(1, 0, kind).start()

    def source_parts():
        both = 2 * PER
        all_of(ga.at[:, :, 1 - c], b_ss.at[1], b_rs.at[2 * NY]).wait_recv()
        a = ga[...].reshape(2 * NY * 2 * both, part_k)
        t = [dot_t(a, w[:, k * part_k : (k + 1) * part_k]).reshape(4 * NY, both, 2 * vec) for k in range(2)]
        c_src[...] = (t[0][:, :PER] + t[1][:, PER:]).reshape(4 * NY * PER, 2 * vec)

    def fs_x(dx):
        xx = lax.rem(x + dx, NX)
        return remote(fs.at[lax.rem(xx, 2), lax.div(xx, 2)], rfs.at[dx - 1], e_ss.at[0], e_rs.at[0], dev(dx=dx))

    def fs_z(k):
        return remote(fss.at[lax.rem(z + k, NZ)], rfsz.at[k], e_ss.at[1], e_rs.at[1], dev(dz=k))

    def fd_z(k):
        return remote(fd.at[lax.rem(z + k, NZ)], rfd.at[k], e_ss.at[2], e_rs.at[2], dev(dz=k))

    def fd_x(dx):
        xx = lax.rem(x + dx, NX)
        return remote(fdd.at[lax.rem(xx, 2), lax.div(xx, 2)], rfdx.at[dx - 1], e_ss.at[3], e_rs.at[3], dev(dx=dx))

    def source_send():
        sums = c_src[...]
        both = 2 * PER
        for pq in range(2):
            for d in range(NY):
                _, yb, slot = place(pq, d)
                r0 = (pq * NY + d) * both
                for g in range(2):
                    fs[lax.rem(yb, 2), g, slot] = sums[r0 : r0 + both, g * vec : (g + 1) * vec]
        for dx in range(1, NX):
            fs_x(dx).start()
        block = jnp.floor((rel[:, 0:1] + 0.5) * (1.0 / (2 * PER)))
        at = rel[:, 0:1] - PER * block
        picked = pick_rows(jnp.where(at == iota((events, events), 1), 1.0, 0.0).astype(BF16), sums)
        for zz in range(NZ):
            for par in range(2):
                r0 = (2 * zz + par) * both
                for g in range(2):
                    fd[zz, par, g] = picked[r0 : r0 + both, g * vec : (g + 1) * vec]
        for k in range(1, NZ):
            fd_z(k).start()

    s_copy = remote(s_out, s_in, p_ss.at[4], p_rs.at[4], dev(dx=2))

    def rows_send():
        here = rel[pl.ds(pl.multiple_of(loop * PER, PER), PER), :]
        there = rel[pl.ds(pl.multiple_of(far_block * PER, PER), PER), :]
        at = jnp.concatenate([here, there], axis=0)[:, 0:1]
        a = ga[...].reshape(8 * NY * PER, part_k)
        for k in range(2):
            onehot = jnp.where(at + k * PER == iota((2 * PER, 8 * NY * PER), 1), 1.0, 0.0).astype(BF16)
            s_out[:, k * part_k : (k + 1) * part_k] = jnp.dot(onehot, a, preferred_element_type=F32).astype(BF16)
        go(s_copy)

    g_out = pltpu.make_async_copy(ng, new_green, in_s.at[3])

    def rows_out():
        s_copy.wait_recv()
        lane16 = iota((rows, 2 * PER), 1)
        put_own = jnp.where(hit & (less == lane16), 1.0, 0.0).astype(BF16)
        put_far = jnp.where(hit & (less + PER == lane16), 1.0, 0.0).astype(BF16)
        keep = jnp.where(jnp.logical_not(hit) & (local_row == iota((rows, rows), 1)), 1.0, 0.0).astype(BF16)
        for cols, put, got in ((own_cols, put_own, s_out), (far_cols, put_far, s_in)):
            ng[:, cols] = (
                jnp.dot(keep, gv[:, cols], preferred_element_type=F32)
                + jnp.dot(put, got[...], preferred_element_type=F32)
            ).astype(BF16)
        g_out.start()

    late = [rfs, rfsz.at[pl.ds(1, NZ - 1)], rfd.at[pl.ds(1, NZ - 1)], rfdx]

    def sources_on():
        all_of(late[0], e_ss.at[0], e_rs.at[0]).wait_recv()
        fss[...] = (fs[xl, h] + rfs[0]) + (rfs[1] + rfs[2])
        for k in range(1, NZ):
            fs_z(k).start()

    def destinations_on():
        all_of(late[2], e_ss.at[2], e_rs.at[2]).wait_recv()
        total = fd[z]
        for k in range(1, NZ):
            total = total + rfd[k]
        fdd[...] = total
        for dx in range(1, NX):
            fd_x(dx).start()

    def takes(*items):
        for item in items:
            take(*item)

    takes((0, -1, 2), (0, 1, 2))
    enter(2)
    takes((0, -1, 0), (0, 1, 1))
    step_near(1)
    enter(0)
    takes((0, -1, 1), (0, 1, 0), (0, -2, 2), (0, 2, 2))
    enter(1)
    step_near(2)
    takes((1, -1, 2), (1, 1, 2), (0, -2, 0), (0, 2, 1), (1, -1, 0), (1, 1, 0))
    step_near(3)
    takes((0, -3, 2), (0, 3, 2), (1, -2, 2), (1, 2, 2), (1, -1, 1), (1, 1, 1), (0, -2, 1), (0, 2, 0))
    c_in.wait()
    h_in.wait_recv()
    compute(0, 0)
    takes((0, 4, 2), (0, 3, 1))
    compute(1, 0)
    takes((1, -3, 2), (1, 3, 2))
    compute(0, -1)
    takes((1, -2, 0), (1, 2, 1))
    compute(0, 1)
    takes((0, -3, 0), (1, 2, 0))
    compute(1, -1)
    takes((1, 4, 2), (1, -2, 1), (0, 3, 0))
    compute(1, 1)
    source_parts()
    source_send()
    takes((0, -3, 1), (1, -3, 0), (1, 3, 1))
    for d in (-2, 2):
        compute(0, d)
    for d in (-2, 2):
        compute(1, d)
    takes((0, 4, 0), (0, 4, 1))
    for d in (-3, 3):
        compute(0, d)
    compute(0, 4)
    takes((1, -3, 1), (1, 3, 0))
    rows_send()
    for d in (0, -1, 1):
        z_stage(0, d)
        z_stage(1, d)
    for d in (-3, 3):
        compute(1, d)
    takes((1, 4, 0), (1, 4, 1))
    compute(1, 4)
    sources_on()
    for d in (-2, 2, -3, 3, 4):
        z_stage(0, d)
        z_stage(1, d)
    destinations_on()
    rows_out()

    wide = 2 * rows
    o_first = (orb * wide).astype(F32)
    o_row = iota((wide, 1), 0)
    in_core = jnp.where(o_row >= rows, 1.0, 0.0)
    o_base, o_abs = o_first + in_core * rows, o_row + o_first
    hit_o, t_less = count(tgt_row, o_base, o_abs)
    hit_i, s_less = count(src_row, o_base, o_abs)
    o_from = o_row - in_core * (rows - kept) - t_less - s_less
    o_from = jnp.where(hit_i > 0.5, two + in_core * PER + s_less, o_from)
    o_from = jnp.where(hit_o > 0.5, two + (2 + in_core) * PER + t_less, o_from)
    order = jnp.where(o_from == iota((wide, wide), 1), 1.0, 0.0).astype(BF16)
    main, from_s, from_d = zs[z], fss[z], fdd[xl, h]
    all_of(late[1], e_ss.at[1], e_rs.at[1]).wait_recv()
    for k in range(1, NZ):
        from_s = from_s + rfsz[k]
    all_of(late[3], e_ss.at[3], e_rs.at[3]).wait_recv()
    for dx in range(1, NX):
        from_d = from_d + rfdx[dx - 1]
    others = pl.ds(1, NZ - 1)
    all_of(rz.at[others], z_ss.at[0], z_rs.at[0]).wait_recv()
    for k in range(1, NZ):
        main = main + rz[k]
    bias[...] = pick_rows(order, jnp.concatenate([main, from_s, from_d], axis=0))

    g_out.wait()
    for copy in started:
        copy.wait_send()
    around = pl.ds(1, NY - 1)
    all_of(ga.at[:, around, c], y_ss.at[2], y_rs.at[0, 0, 0]).wait_send()
    for k in range(2):
        all_of(gb.at[:, around, k, c], y_ss.at[k], y_rs.at[0, 0, 0]).wait_send()
    all_of(ga.at[:, :, c], b_ss.at[1], b_rs.at[0]).wait_send()
    all_of(gb.at[:, :, :, c], b_ss.at[0], b_rs.at[0]).wait_send()
    all_of(rx, x_ss.at[0], x_rs.at[0]).wait_send()
    all_of(rz.at[others], z_ss.at[0], z_rs.at[0]).wait_send()
    for n in range(4):
        all_of(late[n], e_ss.at[n], e_rs.at[n]).wait_send()


def local(cholesky, green_half, partners):
    rows, depth = green_half.shape
    vec = cholesky.shape[0]
    half, kept = depth // 2, rows - 2 * PER
    two, part_k, both = 2 * kept, half // 2, 2 * PER
    dma = pltpu.SemaphoreType.DMA
    vmem = pl.BlockSpec(memory_space=pltpu.VMEM)
    hbm = pl.BlockSpec(memory_space=pl.ANY)
    return pl.pallas_call(
        kernel,
        out_shape=(
            jax.ShapeDtypeStruct((rows, depth), BF16),
            jax.ShapeDtypeStruct((2 * rows, vec), F32),
        ),
        in_specs=[hbm] * 3,
        out_specs=(hbm, vmem),
        scratch_shapes=[
            pltpu.VMEM((rows, depth), BF16),
            pltpu.VMEM((2, 256), jnp.int32),
            pltpu.VMEM((2, NY, 2, both, part_k), BF16),
            pltpu.VMEM((2, NY, 2, 2, kept, part_k), BF16),
            pltpu.VMEM((2 * vec, half), BF16),
            pltpu.VMEM((2, NY, 2, two, vec), F32),
            pltpu.VMEM((3, NZ, two, vec), F32),
            pltpu.VMEM((NZ, two, vec), F32),
            pltpu.VMEM((NZ, two, vec), F32),
            pltpu.VMEM((2, 2, NZ, both, vec), F32),
            pltpu.VMEM((3, NZ, both, vec), F32),
            pltpu.VMEM((NZ, both, vec), F32),
            pltpu.VMEM((NZ, both, vec), F32),
            pltpu.VMEM((NZ, 2, 2, both, vec), F32),
            pltpu.VMEM((NZ, 2, 2, both, vec), F32),
            pltpu.VMEM((2, 2, both, vec), F32),
            pltpu.VMEM((3, both, vec), F32),
            pltpu.VMEM((rows, depth), BF16),
            pltpu.VMEM((both, half), BF16),
            pltpu.VMEM((both, half), BF16),
            pltpu.VMEM((both, part_k), BF16),
            pltpu.VMEM((2, kept, part_k), BF16),
            pltpu.VMEM((256, 2 * vec), F32),
            pltpu.VMEM((256, 128), F32),
            dma((4,)),
            dma((3,)), dma((2, NY, 3)), dma((2,)), dma((2 * NY + 1,)), dma((5,)), dma((5,)),
            dma((1,)), dma((NZ,)), dma((1,)), dma((1,)), dma((4,)), dma((4,)),
            pltpu.SemaphoreType.REGULAR((3,)),
        ],
        compiler_params=pltpu.CompilerParams(
            collective_id=0, has_side_effects=True, vmem_limit_bytes=60 * 1024 * 1024
        ),
    )(cholesky, green_half, partners.T)


def solution(mesh):
    return jax.shard_map(
        local,
        mesh=mesh,
        in_specs=(P("loop", "orb"), P("loop", "orb"), P()),
        out_specs=(P("loop", "orb"), P("orb", "loop")),
        check_vma=False,
    )
```
